1024 devices in a mesh: dp: 128 (over y, z), seq: 8 (over x, core).
Axes of the slice: x: 4, y: 8, z: 16, core: 2. Of those that a mesh axis runs over, the one named last changes fastest.
Arguments:
- section_input: bfloat16 [128, 1024, 1536], P('dp', 'seq'), may hold values from -6 to 6
- lengths: int32 [128], P('dp'), may hold values from 256 to 1024
- depthwise_taps_matrix: float32 [5, 1536], replicated, may hold values from -2.5 to 2.5
- depth_bias: float32 [1536], replicated, may hold values from -3 to 3
- norm_gain: float32 [1536], replicated, may hold values from 0.5 to 1.5
- proj_weight: bfloat16 [768, 1536], replicated, may hold values from -0.15625 to 0.15625
- proj_cotangent: bfloat16 [128, 1024, 768], P('dp', 'seq'), may hold values from -24 to 24
- skip_cotangent: bfloat16 [128, 1024, 1536], P('dp', 'seq'), may hold values from -6 to 6
Outputs:
- input_grad: bfloat16 [128, 1024, 1536], P('dp', 'seq')
- proj_grad: float32 [768, 1536], P('dp', 'seq')
- kernel_grad: float32 [5, 1536], replicated
- bias_grad: float32 [1536], replicated
- gain_grad: float32 [1536], replicated
The draws below stay inside these ranges and needn't reach their ends.
All inputs are finite; a program needn't handle non-finite values.
Results may differ from the reference program's by a relative error of at most 0.0055.
Values may be sent and summed in bfloat16 or wider, within the bound.
A program may use at most 32 MiB of HBM per device.

```python
import jax
import jax.numpy as jnp
from jax import lax

C = 1536
C2 = 768
K = 5
DILATION_STEP = 4
NPOS = 1024
SAMPLES = 128


def place_ends(entries, own_key, low, high):
    longest = entries.shape.index(max(entries.shape))
    spots = []
    for shift in (0, 1):
        where = [jax.random.randint(jax.random.fold_in(own_key, axis), (), 0, length) for axis, length in enumerate(entries.shape)]
        where[longest] = (where[longest] + shift) % entries.shape[longest]
        spots.append(tuple(where))
    return entries.at[spots[0]].set(low).at[spots[1]].set(high)


def strengthened(entries, stream_key, source, target, blocks, factor):
    owner, partner = [(jnp.arange(entries.shape[dim]) // (entries.shape[dim] // blocks)).reshape([-1 if axis == dim else 1 for axis in range(entries.ndim)]) for dim in (source, target)]
    chosen = jax.random.permutation(stream_key, blocks)[partner]
    strong = (owner == chosen) | (owner == (partner + blocks // 2) % blocks)
    return jnp.where(strong, factor * entries, entries)


def levels(rng, extent, shards, smallest, high):
    level = 1.0
    for dim, shards_of in shards:
        draws = jax.random.uniform(jax.random.fold_in(jax.random.fold_in(rng, 6), dim), (shards_of,), jnp.float32, smallest / len(shards), high / len(shards))
        level = level * jnp.repeat(jnp.exp(draws), extent[dim] // shards_of).reshape((-1,) + (1,) * (len(extent) - 1 - dim))
    return level


def noise(stream_key, extent, spread, limit, cuts=(), held_as=jnp.bfloat16):
    values = jax.random.normal(stream_key, extent, jnp.float32) * spread
    if len(cuts) > 0:
        values = levels(stream_key, extent, cuts, -0.22, 0.18) * values
    return jnp.clip(values, min=-limit, max=limit).astype(held_as)


def heavy_noise(rng, extent, deviation, bound, split, heavy, held_as=jnp.bfloat16):
    result = deviation * jax.random.normal(rng, extent, jnp.float32)
    if split:
        result = result * levels(rng, extent, split, -0.22, 0.18)
    return jnp.clip(strengthened(result, jax.random.fold_in(rng, 3), *heavy), -bound, bound).astype(held_as)


def setup_inputs(seed: int = 0) -> dict:
    key_list = jax.random.split(jax.random.key(seed), 9)
    return {
        "section_input": noise(key_list[0], (SAMPLES, NPOS, C), 1.0, 6.0, ((0, 128), (1, 8))),
        "lengths": place_ends(jax.random.randint(key_list[1], (SAMPLES,), NPOS // 4, NPOS + 1), jax.random.fold_in(key_list[1], 1), NPOS // 4, NPOS).astype(jnp.int32),
        "depthwise_taps_matrix": noise(key_list[2], (K, C), K ** -0.5, 2.5, (), jnp.float32),
        "depth_bias": noise(key_list[3], (C,), 0.5, 3.0, (), jnp.float32),
        "norm_gain": jnp.clip(1.0 + 0.1 * jax.random.normal(key_list[4], (C,), jnp.float32), 0.5, 1.5),
        "proj_weight": noise(key_list[5], (C2, C), C ** -0.5, 0.15625),
        "proj_cotangent": heavy_noise(key_list[6], (SAMPLES, NPOS, C2), 1.0, 24.0, ((0, 128), (1, 8)), (0, 2, 128, 5.5)),
        "skip_cotangent": noise(key_list[7], (SAMPLES, NPOS, C), 1.0, 6.0, ((0, 128), (1, 8))),
    }


def norm_gelu(hidden_state, norm_gain):
    inverse = lax.rsqrt(lax.optimization_barrier(jnp.mean(hidden_state * hidden_state, axis=-1, keepdims=True)) + 1e-06)
    return jax.nn.gelu(hidden_state * inverse * norm_gain)

def reference(section_input, lengths, depthwise_taps_matrix, depth_bias, norm_gain, proj_weight, proj_cotangent, skip_cotangent):
    samples = section_input.shape[0]
    position_total = section_input.shape[1]
    channels = section_input.shape[2]
    outputs = proj_cotangent.shape[2]
    kernel_taps = depthwise_taps_matrix.shape[0]
    receptive_reach = kernel_taps // 2 * DILATION_STEP
    positions = jnp.arange(position_total, dtype=jnp.int32)

    def one_sample(carry, item):
        sample_in, length, sample_cot, sample_skip = item
        keep = (positions < length).astype(jnp.bfloat16)[:, None]
        masked = sample_in * keep
        padded_input = jnp.pad(masked.astype(jnp.float32), ((receptive_reach, receptive_reach), (0, 0)))
        hidden_state = jnp.zeros((position_total, channels), jnp.float32) + depth_bias
        for kernel_tap in range(kernel_taps):
            hidden_state = hidden_state + depthwise_taps_matrix[kernel_tap] * padded_input[kernel_tap * DILATION_STEP:kernel_tap * DILATION_STEP + position_total]
        activ, pull = jax.vjp(norm_gelu, hidden_state, norm_gain)
        activ_b = activ.astype(jnp.bfloat16)
        back = jnp.dot(sample_cot, proj_weight, preferred_element_type=jnp.float32) + sample_skip.astype(jnp.float32)
        hidden_grad, gain_part = pull(back)
        grad_b = hidden_grad.astype(jnp.bfloat16)
        gradient_function = grad_b.astype(jnp.float32)
        grad_pad = jnp.pad(gradient_function, ((receptive_reach, receptive_reach), (0, 0)))
        input_grad = jnp.zeros((position_total, channels), jnp.float32)
        for kernel_tap in range(kernel_taps):
            shift_offset = (kernel_taps - 1 - kernel_tap) * DILATION_STEP
            input_grad = input_grad + depthwise_taps_matrix[kernel_tap] * grad_pad[shift_offset:shift_offset + position_total]
        input_grad = (input_grad * keep.astype(jnp.float32)).astype(jnp.bfloat16)
        proj_part = lax.dot_general(sample_cot, activ_b, (((0,), (0,)), ((), ())), preferred_element_type=jnp.float32)
        kernel_partial = jnp.stack([lax.optimization_barrier(jnp.sum(padded_input[kernel_tap * DILATION_STEP:kernel_tap * DILATION_STEP + position_total] * gradient_function, axis=0)) for kernel_tap in range(kernel_taps)])
        bias_part = lax.optimization_barrier(jnp.sum(gradient_function, axis=0))
        proj_sum, kernel_sum, bias_sum, gain_sum = carry
        return ((proj_sum + proj_part, kernel_sum + kernel_partial, bias_sum + bias_part, gain_sum + gain_part), input_grad)
    start = (jnp.zeros((outputs, channels), jnp.float32), jnp.zeros((kernel_taps, channels), jnp.float32), jnp.zeros((channels,), jnp.float32), jnp.zeros((channels,), jnp.float32))
    totals, input_grad = lax.scan(one_sample, start, (section_input, lengths, proj_cotangent, skip_cotangent))
    proj_sum, kernel_sum, bias_sum, gain_sum = totals
    return (input_grad, proj_sum / samples, kernel_sum / samples, bias_sum / samples, gain_sum / samples)
```

```python
import functools

import jax
import jax.numpy as jnp
from jax import lax
from jax.experimental import pallas as pl
from jax.experimental.pallas import tpu as pltpu
from jax.sharding import PartitionSpec as P

STEP = 4
MESH = pl.DeviceIdType.MESH
BLOCK = 16
HALO = 8
XS = 4
LANES = 128
ROOT = 0.7978845608028654
CUBIC = 0.044715

LOC_X, LOC_COT, LOC_SKIP, LOC_W, LOC_OWN, LOC_ACT = range(6)
(S_HALO, S_COT, S_ACT, S_SIB, S_GRAD, S_EX, S_EY, S_EZ, S_EA, S_EF, S_PY, S_PZ) = range(12)
(R_TOP, R_BOT, R_COT, R_ACT1, R_ACT2, R_ACT3, R_SIB, R_GTOP, R_GBOT, R_EX, R_EY, R_EZ, R_EA, R_EF, R_PY, R_PZ) = range(16)


def wait_bytes(ref, sem):
    pltpu.make_async_copy(ref, ref, sem).wait()


def kernel(
    ys,
    zs,
    len_ref,
    x_hbm,
    cot_hbm,
    skip_hbm,
    w_hbm,
    taps_ref,
    bias_ref,
    gain_ref,
    ig_ref,
    pg_ref,
    kg_ref,
    bg_ref,
    gg_ref,
    x_v,
    cot_v,
    skip_v,
    w_v,
    back,
    halo_t,
    halo_b,
    xpad,
    gb,
    ghalo_t,
    ghalo_b,
    gpad,
    eacc,
    cotg,
    actc,
    actg,
    pacc,
    pbuf,
    yrecv,
    tbuf,
    zrecv,
    e_loc,
    e_x,
    e_1,
    e_y,
    e_z,
    e_fin,
    loc,
    snd,
    rcv,
):
    rows, chans = x_v.shape
    outs = cot_v.shape[1]
    half = outs // 2
    quarter = chans // XS
    taps = taps_ref.shape[0]
    samples = ys * zs
    own_rows = outs // samples
    yh, zh = ys // 2, zs // 2
    k_rows = own_rows * zh
    tile = tbuf.shape[2]
    e_rows = e_1.shape[1]

    dp = lax.axis_index("dp")
    s = lax.axis_index("seq")
    y, z = dp // zs, dp % zs
    x, c = s // 2, s % 2
    oc = 1 - c
    sib = 2 * x + oc

    def xat(delta, core):
        return (dp, 2 * ((x + delta) % XS) + core)

    def remote(src, dst, send, recv, device):
        return pltpu.make_async_remote_copy(
            src_ref=src, dst_ref=dst, send_sem=snd.at[send], recv_sem=rcv.at[recv], device_id=device, device_id_type=MESH
        )

    ld_x = pltpu.make_async_copy(x_hbm, x_v, loc.at[LOC_X])
    ld_cot = pltpu.make_async_copy(cot_hbm, cot_v, loc.at[LOC_COT])
    ld_w = pltpu.make_async_copy(w_hbm, w_v, loc.at[LOC_W])
    ld_skip = pltpu.make_async_copy(skip_hbm, skip_v, loc.at[LOC_SKIP])
    my_half = pl.multiple_of(c * half, LANES)
    ld_own = pltpu.make_async_copy(cot_hbm.at[:, pl.ds(my_half, half)], cotg.at[0], loc.at[LOC_OWN])
    ld_x.start()
    ld_cot.start()
    ld_w.start()
    ld_skip.start()
    ld_own.start()

    barrier = pltpu.get_barrier_semaphore()

    def greet(device):
        pl.semaphore_signal(barrier, inc=1, device_id=device, device_id_type=MESH)

    for d in range(1, 2 * XS):
        greet((dp, (s + d) % (2 * XS)))

    def greet_y(d, carry):
        other = ((y + d) % ys) * zs + z
        greet((other, s))
        greet((other, sib))
        return carry

    def greet_z(d, carry):
        other = y * zs + (z + d) % zs
        greet((other, s))
        greet((other, sib))
        return carry

    lax.fori_loop(1, ys, greet_y, 0)
    lax.fori_loop(1, zs, greet_z, 0)
    pl.semaphore_wait(barrier, 2 * XS - 1 + 2 * (ys - 1) + 2 * (zs - 1))

    up, down = (dp, (s + 1) % (2 * XS)), (dp, (s + 2 * XS - 1) % (2 * XS))
    remote(x_hbm.at[pl.ds(rows - BLOCK, BLOCK)], halo_t, S_HALO, R_TOP, up).start()
    remote(x_hbm.at[pl.ds(0, BLOCK)], halo_b, S_HALO, R_BOT, down).start()

    for delta in (1, 3, 2, 0):
        for p in (0, 1):
            if delta == 0 and p == 0:
                continue
            core = c if p == 0 else oc
            start = pl.multiple_of(core * half, LANES)
            remote(
                cot_hbm.at[:, pl.ds(start, half)], cotg.at[4 * p + (XS - delta) % XS], S_COT, R_COT, xat(delta, core)
            ).start()

    length = len_ref[0]
    first = s * rows
    row_id = lax.broadcasted_iota(jnp.int32, (BLOCK, 1), 0)

    ld_cot.wait()
    ld_w.wait()
    ld_skip.wait()

    def back_step(i, carry):
        at = pl.ds(pl.multiple_of(i * quarter, LANES), quarter)
        back[:, at] = jnp.dot(cot_v[...], w_v[:, at], preferred_element_type=jnp.float32) + skip_v[:, at].astype(jnp.float32)
        return carry

    lax.fori_loop(0, XS, back_step, 0)

    ld_x.wait()

    def mask_step(i, carry):
        r0 = pl.multiple_of(i * BLOCK, BLOCK)
        value = x_v[pl.ds(r0, BLOCK), :].astype(jnp.float32)
        xpad[pl.ds(r0 + HALO, BLOCK), :] = jnp.where(first + r0 + row_id < length, value, 0.0)
        return carry

    lax.fori_loop(0, rows // BLOCK, mask_step, 0)
    eacc[...] = jnp.zeros_like(eacc)

    wait_bytes(halo_t, rcv.at[R_TOP])
    wait_bytes(halo_b, rcv.at[R_BOT])
    head_id = first - HALO + lax.broadcasted_iota(jnp.int32, (HALO, 1), 0)
    head = halo_t[...].astype(jnp.float32)[BLOCK - HALO :]
    xpad[0:HALO, :] = jnp.where(jnp.logical_and(head_id >= 0, head_id < length), head, 0.0)
    tail_id = first + rows + lax.broadcasted_iota(jnp.int32, (HALO, 1), 0)
    tail = halo_b[...].astype(jnp.float32)[:HALO]
    xpad[pl.ds(rows + HALO, HALO), :] = jnp.where(
        jnp.logical_and(tail_id < length, s < 2 * XS - 1), tail, 0.0
    )

    def fold(value):
        return value[:HALO] + value[HALO:]

    def shifted(ref, r0):
        even = ref[pl.ds(r0, 2 * BLOCK), :]
        odd = even[STEP : STEP + BLOCK + HALO]
        return [even[:BLOCK], odd[:BLOCK], even[HALO : HALO + BLOCK], odd[HALO:], even[BLOCK:]]

    def main_step(i, carry):
        r0 = pl.multiple_of(i * BLOCK, BLOCK)
        seen = shifted(xpad, r0)
        hidden = bias_ref[...] + taps_ref[0:1, :] * seen[0]
        for j in range(1, taps):
            hidden = hidden + taps_ref[j : j + 1, :] * seen[j]
        inverse = lax.rsqrt(jnp.mean(hidden * hidden, axis=-1, keepdims=True) + 1e-06)
        normed = hidden * inverse
        gain = gain_ref[...]
        u = normed * gain
        square = u * u
        tanh = jnp.tanh(u * (ROOT + ROOT * CUBIC * square))
        cdf = 0.5 + 0.5 * tanh
        act = (u * cdf).astype(jnp.bfloat16)
        for q in range(XS):
            actc[q, pl.ds(r0, BLOCK), :] = act[:, q * quarter : (q + 1) * quarter]
        slope = cdf + u * (1.0 - tanh * tanh) * (0.5 * ROOT + 1.5 * ROOT * CUBIC * square)
        toward = back[pl.ds(r0, BLOCK), :] * slope
        eacc[pl.ds((taps + 1) * HALO, HALO), :] += fold(toward * normed)
        toward = toward * gain
        pull = jnp.mean(toward * normed, axis=-1, keepdims=True)
        grad = ((toward - normed * pull) * inverse).astype(jnp.bfloat16)
        gb[pl.ds(r0, BLOCK), :] = grad
        grad = grad.astype(jnp.float32)
        gpad[pl.ds(r0 + HALO, BLOCK), :] = grad
        eacc[pl.ds(taps * HALO, HALO), :] += fold(grad)
        for j in range(taps):
            eacc[pl.ds(j * HALO, HALO), :] += fold(grad * seen[j])
        return carry

    lax.fori_loop(0, rows // BLOCK, main_step, 0)

    for delta in (1, 3, 2):
        remote(
            actc.at[(x + delta) % XS], actg.at[XS - delta], S_ACT, R_ACT1 + (XS - delta) - 1, xat(delta, c)
        ).start()
    remote(actc.at[x], actg.at[4], S_SIB, R_SIB, (dp, sib)).start()
    own_act = pltpu.make_async_copy(actc.at[x], actg.at[0], loc.at[LOC_ACT])
    own_act.start()

    remote(gb.at[pl.ds(rows - BLOCK, BLOCK)], ghalo_t, S_GRAD, R_GTOP, up).start()
    remote(gb.at[pl.ds(0, BLOCK)], ghalo_b, S_GRAD, R_GBOT, down).start()

    for r in range(taps + 2):
        line = jnp.sum(eacc[r * HALO : (r + 1) * HALO, :], axis=0, keepdims=True)
        for q in range(XS):
            e_loc[q, r : r + 1, :] = line[:, q * quarter : (q + 1) * quarter]
    for q in range(XS):
        e_loc[q, taps + 2 :, :] = jnp.zeros((HALO - taps - 2, quarter), jnp.float32)
    for delta in (1, 3, 2):
        remote(e_loc.at[(x + delta) % XS], e_x.at[XS - delta - 1], S_EX, R_EX, xat(delta, c)).start()

    wait_bytes(ghalo_t, rcv.at[R_GTOP])
    wait_bytes(ghalo_b, rcv.at[R_GBOT])
    gpad[0:HALO, :] = jnp.where(s > 0, ghalo_t[...].astype(jnp.float32)[BLOCK - HALO :], 0.0)
    gpad[pl.ds(rows + HALO, HALO), :] = jnp.where(s < 2 * XS - 1, ghalo_b[...].astype(jnp.float32)[:HALO], 0.0)

    def input_step(i, carry):
        r0 = pl.multiple_of(i * BLOCK, BLOCK)
        seen = shifted(gpad, r0)
        total = taps_ref[0:1, :] * seen[taps - 1]
        for j in range(1, taps):
            total = total + taps_ref[j : j + 1, :] * seen[taps - 1 - j]
        ig_ref[pl.ds(r0, BLOCK), :] = jnp.where(first + r0 + row_id < length, total, 0.0).astype(jnp.bfloat16)
        return carry

    lax.fori_loop(0, rows // BLOCK, input_step, 0)

    wait_bytes(e_x, rcv.at[R_EX])
    e_sum = e_loc[x] + e_x[0] + e_x[1] + e_x[2]
    for r in range(HALO):
        e_1[r // e_rows, r % e_rows : r % e_rows + 1, :] = e_sum[r : r + 1]
    for d in range(1, ys):
        other = (y + d) % ys
        remote(e_1.at[other], e_y.at[ys - d - 1], S_EY, R_EY, (other * zs + z, s)).start()

    wait_bytes(cotg.at[pl.ds(1, 7)], rcv.at[R_COT])
    ld_own.wait()
    for d in (3, 1, 2):
        wait_bytes(actg.at[d], rcv.at[R_ACT1 + d - 1])
        remote(actg.at[d], actg.at[4 + d], S_SIB, R_SIB, (dp, sib)).start()
    own_act.wait()

    def product(at):
        a = cotg[at : at + 4].reshape(4 * rows, half)
        b = actg[at : at + 4].reshape(4 * rows, quarter)
        return lax.dot_general(a, b, (((0,), (0,)), ((), ())), preferred_element_type=jnp.float32)

    pacc[...] = product(0)

    wait_bytes(e_y, rcv.at[R_EY])
    e_row = e_1[y]
    for d in range(ys - 1):
        e_row = e_row + e_y[d]
    e_z[z] = e_row
    for d in range(1, zs):
        remote(e_z.at[z], e_z.at[z], S_EZ, R_EZ, (y * zs + (z + d) % zs, s)).start()

    wait_bytes(actg.at[pl.ds(4, 4)], rcv.at[R_SIB])
    part = (pacc[...] + product(4)).astype(jnp.bfloat16)
    for i in range(ys):
        pbuf[i] = part[i * k_rows : (i + 1) * k_rows]

    for i in range(yh):
        for k in range(2):
            other = yh * c + i
            slot = (y + ys - other) % ys
            mine = jnp.logical_and(other == y, c == k)

            @pl.when(mine)
            def _():
                yrecv[0] = pbuf[2 * i + k]

            @pl.when(jnp.logical_not(mine))
            def _():
                remote(pbuf.at[2 * i + k], yrecv.at[slot], S_PY, R_PY, (other * zs + z, 2 * x + k)).start()

    wait_bytes(e_z.at[pl.ds(0, zs - 1)], rcv.at[R_EZ])
    e_row = e_z[0]
    for d in range(1, zs):
        e_row = e_row + e_z[d]
    e_fin[s, y] = e_row
    for d in range(1, ys):
        remote(e_fin.at[s, y], e_fin.at[s, y], S_EA, R_EA, (((y + d) % ys) * zs + z, s)).start()

    own_y = y // yh == c

    @pl.when(own_y)
    def _():
        wait_bytes(yrecv.at[pl.ds(0, ys - 1)], rcv.at[R_PY])

    @pl.when(jnp.logical_not(own_y))
    def _():
        wait_bytes(yrecv, rcv.at[R_PY])

    total = yrecv[0].astype(jnp.float32)
    for d in range(1, ys):
        total = total + yrecv[d].astype(jnp.float32)
    total = total.astype(jnp.bfloat16)
    sel_row = lax.broadcasted_iota(jnp.int32, (zh * tile, k_rows), 0)
    sel_col = lax.broadcasted_iota(jnp.int32, (zh * tile, k_rows), 1)
    within = sel_row % tile
    base = (sel_row // tile) * own_rows
    pick_a = jnp.logical_and(within < own_rows, sel_col == base + within).astype(jnp.bfloat16)
    low = within - tile // 2
    pick_b = jnp.logical_and(jnp.logical_and(low >= 0, low < own_rows), sel_col == base + low).astype(jnp.bfloat16)
    middle = jnp.dot(pick_b, total[:, LANES : 2 * LANES], preferred_element_type=jnp.float32)
    for q in range(2):
        outer = jnp.dot(pick_a, total[:, 2 * LANES * q : 2 * LANES * q + LANES], preferred_element_type=jnp.float32)
        both = (outer + middle).astype(jnp.bfloat16)
        for j in range(zh):
            tbuf[j, q] = both[j * tile : (j + 1) * tile]
    for j in range(zh):
        for q in range(2):
            other = zh * c + j
            slot = (z + zs - other) % zs
            mine = jnp.logical_and(other == z, c == q)

            @pl.when(mine)
            def _():
                zrecv[0] = tbuf[j, q]

            @pl.when(jnp.logical_not(mine))
            def _():
                remote(tbuf.at[j, q], zrecv.at[slot], S_PZ, R_PZ, (y * zs + other, 2 * x + q)).start()

    wait_bytes(e_fin.at[0, pl.ds(0, ys - 1)], rcv.at[R_EA])
    for d in range(1, 2 * XS):
        remote(e_fin.at[s], e_fin.at[s], S_EF, R_EF, (dp, (s + d) % (2 * XS))).start()

    own_z = z // zh == c

    @pl.when(own_z)
    def _():
        wait_bytes(zrecv.at[pl.ds(0, zs - 1)], rcv.at[R_PZ])

    @pl.when(jnp.logical_not(own_z))
    def _():
        wait_bytes(zrecv, rcv.at[R_PZ])

    final = zrecv[0].astype(jnp.float32)
    for d in range(1, zs):
        final = final + zrecv[d].astype(jnp.float32)
    final = final / samples
    side = final[:own_rows]
    inner = final[tile // 2 : tile // 2 + own_rows]
    cut = quarter // 2 - LANES
    first_half = jnp.concatenate([side, inner[:, :cut]], axis=1)
    second_half = jnp.concatenate([inner[:, cut:], side], axis=1)
    pg_ref[...] = jnp.where(c == 0, first_half, second_half)

    wait_bytes(e_fin.at[pl.ds(0, 2 * XS - 1)], rcv.at[R_EF])
    for q in range(XS):
        at = slice(q * quarter, (q + 1) * quarter)
        for r in range(taps + 2):
            line = (e_fin[2 * q, r // e_rows, r % e_rows : r % e_rows + 1] + e_fin[2 * q + 1, r // e_rows, r % e_rows : r % e_rows + 1]) / samples
            if r < taps:
                kg_ref[r : r + 1, at] = line
            elif r == taps:
                bg_ref[:, at] = line
            else:
                gg_ref[:, at] = line

    wait_bytes(x_v.at[pl.ds(0, 2 * BLOCK)], snd.at[S_HALO])
    wait_bytes(cotg.at[pl.ds(0, 7)], snd.at[S_COT])
    wait_bytes(actg.at[pl.ds(0, 3)], snd.at[S_ACT])
    wait_bytes(actg.at[pl.ds(0, 4)], snd.at[S_SIB])
    wait_bytes(gb.at[pl.ds(0, 2 * BLOCK)], snd.at[S_GRAD])
    wait_bytes(e_x, snd.at[S_EX])
    wait_bytes(e_y, snd.at[S_EY])
    wait_bytes(e_z.at[pl.ds(0, zs - 1)], snd.at[S_EZ])
    wait_bytes(e_fin.at[0, pl.ds(0, ys - 1)], snd.at[S_EA])
    wait_bytes(e_fin.at[pl.ds(0, 2 * XS - 1)], snd.at[S_EF])

    @pl.when(own_y)
    def _():
        wait_bytes(pbuf.at[pl.ds(0, ys - 1)], snd.at[S_PY])

    @pl.when(jnp.logical_not(own_y))
    def _():
        wait_bytes(pbuf, snd.at[S_PY])

    @pl.when(own_z)
    def _():
        wait_bytes(zrecv.at[pl.ds(0, zs - 1)], snd.at[S_PZ])

    @pl.when(jnp.logical_not(own_z))
    def _():
        wait_bytes(zrecv, snd.at[S_PZ])


def shards(ys, zs, section, lengths, taps, bias, gain, weight, cot, skip):
    samp, rows, chans = section.shape
    outs = cot.shape[2]
    half, quarter = outs // 2, chans // XS
    samples = ys * zs
    own_rows = outs // samples
    k_rows = own_rows * (zs // 2)
    tile = 2 * (-(-own_rows // 8) * 8)
    e_rows = HALO // ys
    kinds = taps.shape[0]
    bf16, f32 = jnp.bfloat16, jnp.float32
    vmem = pl.BlockSpec(memory_space=pltpu.VMEM)
    anywhere = pl.BlockSpec(memory_space=pl.ANY)
    result = pl.pallas_call(
        functools.partial(kernel, ys, zs),
        out_shape=(
            jax.ShapeDtypeStruct((rows, chans), bf16),
            jax.ShapeDtypeStruct((own_rows, quarter // 2), f32),
            jax.ShapeDtypeStruct((kinds, chans), f32),
            jax.ShapeDtypeStruct((1, chans), f32),
            jax.ShapeDtypeStruct((1, chans), f32),
        ),
        in_specs=[pl.BlockSpec(memory_space=pltpu.SMEM), anywhere, anywhere, anywhere, anywhere, vmem, vmem, vmem],
        out_specs=(vmem,) * 5,
        scratch_shapes=[
            pltpu.VMEM((rows, chans), bf16),
            pltpu.VMEM((rows, outs), bf16),
            pltpu.VMEM((rows, chans), bf16),
            pltpu.VMEM((outs, chans), bf16),
            pltpu.VMEM((rows, chans), f32),
            pltpu.VMEM((BLOCK, chans), bf16),
            pltpu.VMEM((BLOCK, chans), bf16),
            pltpu.VMEM((rows + 2 * HALO, chans), f32),
            pltpu.VMEM((rows, chans), bf16),
            pltpu.VMEM((BLOCK, chans), bf16),
            pltpu.VMEM((BLOCK, chans), bf16),
            pltpu.VMEM((rows + 2 * HALO, chans), f32),
            pltpu.VMEM(((kinds + 2) * HALO, chans), f32),
            pltpu.VMEM((8, rows, half), bf16),
            pltpu.VMEM((XS, rows, quarter), bf16),
            pltpu.VMEM((8, rows, quarter), bf16),
            pltpu.VMEM((half, quarter), f32),
            pltpu.VMEM((ys, k_rows, quarter), bf16),
            pltpu.VMEM((ys, k_rows, quarter), bf16),
            pltpu.VMEM((zs // 2, 2, tile, LANES), bf16),
            pltpu.VMEM((zs, tile, LANES), bf16),
            pltpu.VMEM((XS, HALO, quarter), f32),
            pltpu.VMEM((XS - 1, HALO, quarter), f32),
            pltpu.VMEM((ys, e_rows, quarter), f32),
            pltpu.VMEM((ys - 1, e_rows, quarter), f32),
            pltpu.VMEM((zs, e_rows, quarter), f32),
            pltpu.VMEM((2 * XS, ys, e_rows, quarter), f32),
            pltpu.SemaphoreType.DMA((6,)),
            pltpu.SemaphoreType.DMA((12,)),
            pltpu.SemaphoreType.DMA((16,)),
        ],
        compiler_params=pltpu.CompilerParams(collective_id=0, has_side_effects=True, vmem_limit_bytes=48 * 1024 * 1024),
        cost_estimate=pl.CostEstimate(flops=4 * rows * outs * chans, bytes_accessed=4_000_000, transcendentals=rows * chans),
    )(
        lengths,
        section.reshape(rows, chans),
        cot.reshape(rows, outs),
        skip.reshape(rows, chans),
        weight,
        taps,
        bias.reshape(1, chans),
        gain.reshape(1, chans),
    )
    input_grad, proj, taps_grad, bias_grad, gain_grad = result
    return input_grad.reshape(section.shape), proj, taps_grad, bias_grad.reshape(chans), gain_grad.reshape(chans)


def solution(mesh):
    dp = mesh.shape["dp"]
    ys = 8 if dp == 128 else 2
    in_specs = (
        P("dp", "seq", None),
        P("dp"),
        P(),
        P(),
        P(),
        P(),
        P("dp", "seq", None),
        P("dp", "seq", None),
    )
    out_specs = (P("dp", "seq", None), P("dp", "seq"), P(), P(), P())
    return jax.shard_map(
        functools.partial(shards, ys, dp // ys), mesh=mesh, in_specs=in_specs, out_specs=out_specs, check_vma=False
    )
```

```python
import functools

import jax
import jax.numpy as jnp
from jax import lax
from jax.experimental import pallas as pl
from jax.experimental.pallas import tpu as pltpu
from jax.sharding import PartitionSpec as P

STEP = 4
MESH = pl.DeviceIdType.MESH
BLOCK = 16
HALO = 8
XS = 4
LANES = 128
ROOT = 0.7978845608028654
CUBIC = 0.044715

LOC_X, LOC_COT, LOC_SKIP, LOC_W, LOC_OWN, LOC_ACT, LOC_LEN, LOC_TAPS, LOC_BIAS, LOC_GAIN, LOC_IG = range(11)
(S_HALO, S_COT, S_FWD, S_ACT, S_SIB, S_GRAD, S_EX, S_EY, S_EZ, S_EA, S_EF, S_PZ) = range(12)
(R_TOP, R_BOT, R_COTS, R_COT1, R_COT2, R_COT3, R_GTOP, R_GBOT, R_EX, R_EY, R_EZ, R_EA, R_EF, R_PZ) = range(14)
S_PY = 12
R_ACT, R_SIB, R_PY = 14, 23, 26
CHUNKS = 3
ORDER = (1, 0, 2)


def wait_bytes(ref, sem):
    pltpu.make_async_copy(ref, ref, sem).wait()


def kernel(
    ys,
    zs,
    len_hbm,
    x_hbm,
    cot_hbm,
    skip_hbm,
    w_hbm,
    taps_hbm,
    bias_hbm,
    gain_hbm,
    ig_ref,
    pg_ref,
    kg_ref,
    bg_ref,
    gg_ref,
    len_ref,
    taps_ref,
    bias_ref,
    gain_ref,
    x_v,
    cot_v,
    skip_v,
    w_v,
    back,
    halo_t,
    halo_b,
    xpad,
    gb,
    ig_v,
    ghalo_t,
    ghalo_b,
    gpad,
    eacc,
    cotg,
    cott,
    actc,
    actg,
    pacc,
    pbuf,
    yrecv,
    tbuf,
    zrecv,
    e_loc,
    e_x,
    e_1,
    e_y,
    e_z,
    e_fin,
    loc,
    snd,
    rcv,
    ysem,
    zsem,
):
    rows, chans = x_v.shape
    outs = cot_v.shape[1]
    half = outs // 2
    quarter = chans // XS
    taps = taps_ref.shape[0]
    samples = ys * zs
    own_rows = outs // samples
    yh, zh = ys // 2, zs // 2
    k_rows = own_rows * zh
    tile = tbuf.shape[2]
    e_rows = e_1.shape[1]

    dp = lax.axis_index("dp")
    s = lax.axis_index("seq")
    y, z = dp // zs, dp % zs
    x, c = s // 2, s % 2
    oc = 1 - c
    sib = 2 * x + oc

    def xat(delta, core):
        return (dp, 2 * ((x + delta) % XS) + core)

    def remote(src, dst, send, recv, device):
        return pltpu.make_async_remote_copy(
            src_ref=src, dst_ref=dst, send_sem=snd.at[send], recv_sem=rcv.at[recv], device_id=device, device_id_type=MESH
        )

    ld_x = pltpu.make_async_copy(x_hbm, x_v, loc.at[LOC_X])
    ld_cot = pltpu.make_async_copy(cot_hbm, cot_v, loc.at[LOC_COT])
    ld_w = pltpu.make_async_copy(w_hbm, w_v, loc.at[LOC_W])
    ld_skip = pltpu.make_async_copy(skip_hbm, skip_v, loc.at[LOC_SKIP])
    my_half = pl.multiple_of(c * half, LANES)
    ld_own = pltpu.make_async_copy(cot_hbm.at[:, pl.ds(my_half, half)], cotg.at[0], loc.at[LOC_OWN])
    ld_x.start()
    ld_cot.start()
    ld_w.start()
    ld_skip.start()
    ld_own.start()
    ld_len = pltpu.make_async_copy(len_hbm, len_ref, loc.at[LOC_LEN])
    ld_taps = pltpu.make_async_copy(taps_hbm, taps_ref, loc.at[LOC_TAPS])
    ld_bias = pltpu.make_async_copy(bias_hbm, bias_ref, loc.at[LOC_BIAS])
    ld_gain = pltpu.make_async_copy(gain_hbm, gain_ref, loc.at[LOC_GAIN])
    ld_len.start()
    ld_taps.start()
    ld_bias.start()
    ld_gain.start()

    barrier = pltpu.get_barrier_semaphore()
    for d in range(1, 2 * XS):
        pl.semaphore_signal(barrier, inc=1, device_id=(dp, (s + d) % (2 * XS)), device_id_type=MESH)
    y_steps = (1, ys - 1) if ys > 2 else (1,)
    z_steps = (1, zs - 1) if zs > 2 else (1,)
    for d in y_steps:
        for device in (s, sib):
            pl.semaphore_signal(barrier, inc=1, device_id=(((y + d) % ys) * zs + z, device), device_id_type=MESH)
    for d in z_steps:
        for device in (s, sib):
            pl.semaphore_signal(barrier, inc=1, device_id=(y * zs + (z + d) % zs, device), device_id_type=MESH)
    pl.semaphore_wait(barrier, 2 * XS - 1 + 2 * (1 if ys == 2 else 2) + 2 * (1 if zs == 2 else 2))

    reach_y = (1, 2) if ys == 8 else ()
    reach_z = (1, 2, 4) if zs == 16 else (1,) if zs == 4 else ()

    def tell(i):
        if i < len(reach_y):
            for d in (reach_y[i], ys - reach_y[i]):
                pl.semaphore_signal(ysem.at[i], inc=1, device_id=(((y + d) % ys) * zs + z, s), device_id_type=MESH)
        if i < len(reach_z):
            for d in (reach_z[i], zs - reach_z[i]):
                pl.semaphore_signal(zsem.at[i], inc=1, device_id=(y * zs + (z + d) % zs, s), device_id_type=MESH)

    def hear(i):
        if i < len(reach_y):
            pl.semaphore_wait(ysem.at[i], 2)
        if i < len(reach_z):
            pl.semaphore_wait(zsem.at[i], 2)

    up, down = (dp, (s + 1) % (2 * XS)), (dp, (s + 2 * XS - 1) % (2 * XS))
    remote(x_hbm.at[pl.ds(rows - BLOCK, BLOCK)], halo_t, S_HALO, R_TOP, up).start()
    remote(x_hbm.at[pl.ds(0, BLOCK)], halo_b, S_HALO, R_BOT, down).start()

    for delta, recv in ((1, R_COT3), (3, R_COT1), (0, R_COTS)):
        for p in (0, 1):
            if delta == 0 and p == 0:
                continue
            core = c if p == 0 else oc
            start = pl.multiple_of(core * half, LANES)
            remote(
                cot_hbm.at[:, pl.ds(start, half)], cotg.at[4 * p + (XS - delta) % XS], S_COT, recv, xat(delta, core)
            ).start()
    tell(0)

    ld_len.wait()
    length = len_ref[0]
    first = s * rows
    row_id = lax.broadcasted_iota(jnp.int32, (BLOCK, 1), 0)

    ld_cot.wait()
    ld_w.wait()
    ld_skip.wait()

    def back_step(i, carry):
        at = pl.ds(pl.multiple_of(i * quarter, LANES), quarter)
        back[:, at] = jnp.dot(cot_v[...], w_v[:, at], preferred_element_type=jnp.float32) + skip_v[:, at].astype(jnp.float32)
        return carry

    hear(0)
    tell(1)
    lax.fori_loop(0, XS, back_step, 0)

    ld_x.wait()
    ld_taps.wait()
    ld_bias.wait()
    ld_gain.wait()

    def mask_step(i, carry):
        r0 = pl.multiple_of(i * BLOCK, BLOCK)
        value = x_v[pl.ds(r0, BLOCK), :].astype(jnp.float32)
        xpad[pl.ds(r0 + HALO, BLOCK), :] = jnp.where(first + r0 + row_id < length, value, 0.0)
        return carry

    lax.fori_loop(0, rows // BLOCK, mask_step, 0)
    eacc[...] = jnp.zeros_like(eacc)

    wait_bytes(halo_t, rcv.at[R_TOP])
    wait_bytes(halo_b, rcv.at[R_BOT])
    head_id = first - HALO + lax.broadcasted_iota(jnp.int32, (HALO, 1), 0)
    head = halo_t[...].astype(jnp.float32)[BLOCK - HALO :]
    xpad[0:HALO, :] = jnp.where(jnp.logical_and(head_id >= 0, head_id < length), head, 0.0)
    tail_id = first + rows + lax.broadcasted_iota(jnp.int32, (HALO, 1), 0)
    tail = halo_b[...].astype(jnp.float32)[:HALO]
    xpad[pl.ds(rows + HALO, HALO), :] = jnp.where(
        jnp.logical_and(tail_id < length, s < 2 * XS - 1), tail, 0.0
    )

    def fold(value):
        return value[:HALO] + value[HALO:]

    def shifted(ref, r0):
        even = ref[pl.ds(r0, 2 * BLOCK), :]
        odd = even[STEP : STEP + BLOCK + HALO]
        return [even[:BLOCK], odd[:BLOCK], even[HALO : HALO + BLOCK], odd[HALO:], even[BLOCK:]]

    def main_step(i, carry):
        r0 = pl.multiple_of(i * BLOCK, BLOCK)
        seen = shifted(xpad, r0)
        hidden = bias_ref[...].reshape(1, chans) + taps_ref[0:1, :] * seen[0]
        for j in range(1, taps):
            hidden = hidden + taps_ref[j : j + 1, :] * seen[j]
        inverse = lax.rsqrt(jnp.mean(hidden * hidden, axis=-1, keepdims=True) + 1e-06)
        normed = hidden * inverse
        gain = gain_ref[...].reshape(1, chans)
        u = normed * gain
        square = u * u
        tanh = jnp.tanh(u * (ROOT + ROOT * CUBIC * square))
        cdf = 0.5 + 0.5 * tanh
        act = (u * cdf).astype(jnp.bfloat16)
        for m in range(XS * CHUNKS):
            actc[m, pl.ds(r0, BLOCK), :] = act[:, m * LANES : (m + 1) * LANES]
        slope = cdf + u * (1.0 - tanh * tanh) * (0.5 * ROOT + 1.5 * ROOT * CUBIC * square)
        toward = back[pl.ds(r0, BLOCK), :] * slope
        eacc[pl.ds((taps + 1) * HALO, HALO), :] += fold(toward * normed)
        toward = toward * gain
        pull = jnp.mean(toward * normed, axis=-1, keepdims=True)
        grad = ((toward - normed * pull) * inverse).astype(jnp.bfloat16)
        gb[pl.ds(r0, BLOCK), :] = grad
        grad = grad.astype(jnp.float32)
        gpad[pl.ds(r0 + HALO, BLOCK), :] = grad
        eacc[pl.ds(taps * HALO, HALO), :] += fold(grad)
        for j in range(taps):
            eacc[pl.ds(j * HALO, HALO), :] += fold(grad * seen[j])
        return carry

    lax.fori_loop(0, rows // BLOCK, main_step, 0)

    for r in range(taps + 2):
        line = jnp.sum(eacc[r * HALO : (r + 1) * HALO, :], axis=0, keepdims=True)
        for q in range(XS):
            e_loc[q, r : r + 1, :] = line[:, q * quarter : (q + 1) * quarter]
    for q in range(XS):
        e_loc[q, taps + 2 :, :] = jnp.zeros((HALO - taps - 2, quarter), jnp.float32)
    for delta in (2, 1, 3):
        remote(e_loc.at[(x + delta) % XS], e_x.at[XS - delta - 1], S_EX, R_EX, xat(delta, c)).start()

    remote(gb.at[pl.ds(rows - BLOCK, BLOCK)], ghalo_t, S_GRAD, R_GTOP, up).start()
    remote(gb.at[pl.ds(0, BLOCK)], ghalo_b, S_GRAD, R_GBOT, down).start()

    part = rows // 2
    wait_bytes(cotg.at[pl.ds(0, 2)], rcv.at[R_COT3])
    for p in (0, 1):
        at = pl.ds(0, part)
        remote(cotg.at[4 * p + 3, at], cotg.at[4 * p + 2, at], S_FWD, R_COT2, xat(1, c)).start()
    wait_bytes(cotg.at[pl.ds(0, 2)], rcv.at[R_COT1])
    for p in (0, 1):
        at = pl.ds(part, part)
        remote(cotg.at[4 * p + 1, at], cotg.at[4 * p + 2, at], S_FWD, R_COT2, xat(3, c)).start()

    for k in ORDER:
        for delta in (2, 1, 3):
            slot = XS - delta
            remote(
                actc.at[CHUNKS * ((x + delta) % XS) + k], actg.at[k, slot], S_ACT, R_ACT + 3 * k + slot - 1, xat(delta, c)
            ).start()
        remote(actc.at[CHUNKS * x + k], actg.at[k, 4], S_SIB, R_SIB + k, (dp, sib)).start()
        pltpu.make_async_copy(actc.at[CHUNKS * x + k], actg.at[k, 0], loc.at[LOC_ACT]).start()
    hear(1)
    tell(2)

    def turn(slot):
        cott[:, slot * rows : (slot + 1) * rows] = jnp.transpose(cotg[slot])

    ld_own.wait()
    wait_bytes(cotg.at[0], rcv.at[R_COTS])
    for slot in (0, 4, 1, 5, 3, 7):
        turn(slot)

    wait_bytes(ghalo_t, rcv.at[R_GTOP])
    wait_bytes(ghalo_b, rcv.at[R_GBOT])
    gpad[0:HALO, :] = jnp.where(s > 0, ghalo_t[...].astype(jnp.float32)[BLOCK - HALO :], 0.0)
    gpad[pl.ds(rows + HALO, HALO), :] = jnp.where(s < 2 * XS - 1, ghalo_b[...].astype(jnp.float32)[:HALO], 0.0)

    def input_step(i, carry):
        r0 = pl.multiple_of(i * BLOCK, BLOCK)
        seen = shifted(gpad, r0)
        total = taps_ref[0:1, :] * seen[taps - 1]
        for j in range(1, taps):
            total = total + taps_ref[j : j + 1, :] * seen[taps - 1 - j]
        ig_v[pl.ds(r0, BLOCK), :] = jnp.where(first + r0 + row_id < length, total, 0.0).astype(jnp.bfloat16)
        return carry

    lax.fori_loop(0, rows // BLOCK, input_step, 0)
    put_ig = pltpu.make_async_copy(ig_v, ig_ref, loc.at[LOC_IG])
    put_ig.start()
    hear(2)

    wait_bytes(e_x, rcv.at[R_EX])
    e_sum = e_loc[x] + e_x[0] + e_x[1] + e_x[2]
    for r in range(HALO):
        e_1[r // e_rows, r % e_rows : r % e_rows + 1, :] = e_sum[r : r + 1]
    for d in range(1, ys):
        other = (y + d) % ys
        remote(e_1.at[other], e_y.at[ys - d - 1], S_EY, R_EY, (other * zs + z, s)).start()

    wait_bytes(cotg.at[pl.ds(0, 2)], rcv.at[R_COT2])
    turn(2)
    turn(6)
    wait_bytes(actc.at[pl.ds(0, CHUNKS)], loc.at[LOC_ACT])

    def same_parity(k):
        for d in (1, 3, 2):
            wait_bytes(actg.at[k, d], rcv.at[R_ACT + 3 * k + d - 1])
            remote(actg.at[k, d], actg.at[k, 4 + d], S_SIB, R_SIB + k, (dp, sib)).start()
        pacc[k] = jnp.dot(
            cott[:, : 4 * rows], actg[k, 0:4].reshape(4 * rows, LANES), preferred_element_type=jnp.float32
        )

    def other_parity(k):
        wait_bytes(actg.at[k, pl.ds(4, 4)], rcv.at[R_SIB + k])
        whole = pacc[k] + jnp.dot(
            cott[:, 4 * rows :], actg[k, 4:8].reshape(4 * rows, LANES), preferred_element_type=jnp.float32
        )
        whole = whole.astype(jnp.bfloat16)
        for i in range(ys):
            pbuf[k, i] = whole[i * k_rows : (i + 1) * k_rows]
        for i in range(yh):
            for core in range(2):
                other = yh * c + i
                slot = (y + ys - other) % ys
                mine = jnp.logical_and(other == y, c == core)

                @pl.when(mine)
                def _():
                    yrecv[k, 0] = pbuf[k, 2 * i + core]

                @pl.when(jnp.logical_not(mine))
                def _():
                    remote(
                        pbuf.at[k, 2 * i + core], yrecv.at[k, slot], S_PY + k, R_PY + k, (other * zs + z, 2 * x + core)
                    ).start()

    same_parity(ORDER[0])
    same_parity(ORDER[1])
    other_parity(ORDER[0])
    same_parity(ORDER[2])
    other_parity(ORDER[1])
    other_parity(ORDER[2])

    wait_bytes(e_y, rcv.at[R_EY])
    e_row = e_1[y]
    for d in range(ys - 1):
        e_row = e_row + e_y[d]
    e_z[z] = e_row
    for d in range(1, zs):
        remote(e_z.at[z], e_z.at[z], S_EZ, R_EZ, (y * zs + (z + d) % zs, s)).start()

    own_y = y // yh == c
    sel_row = lax.broadcasted_iota(jnp.int32, (zh * tile, k_rows), 0)
    sel_col = lax.broadcasted_iota(jnp.int32, (zh * tile, k_rows), 1)
    within = sel_row % tile
    base = (sel_row // tile) * own_rows
    pick_a = jnp.logical_and(within < own_rows, sel_col == base + within).astype(jnp.bfloat16)
    low = within - tile // 2
    pick_b = jnp.logical_and(jnp.logical_and(low >= 0, low < own_rows), sel_col == base + low).astype(jnp.bfloat16)

    def over_y(k, pick):
        @pl.when(own_y)
        def _():
            wait_bytes(yrecv.at[k, pl.ds(0, ys - 1)], rcv.at[R_PY + k])

        @pl.when(jnp.logical_not(own_y))
        def _():
            wait_bytes(yrecv.at[k], rcv.at[R_PY + k])

        total = yrecv[k, 0].astype(jnp.float32)
        for d in range(1, ys):
            total = total + yrecv[k, d].astype(jnp.float32)
        return jnp.dot(pick, total.astype(jnp.bfloat16), preferred_element_type=jnp.float32)

    middle = over_y(1, pick_b)
    for q in range(2):
        both = (over_y(2 * q, pick_a) + middle).astype(jnp.bfloat16)
        for j in range(zh):
            tbuf[j, q] = both[j * tile : (j + 1) * tile]
        for j in range(zh):
            other = zh * c + j
            slot = (z + zs - other) % zs
            mine = jnp.logical_and(other == z, c == q)

            @pl.when(mine)
            def _():
                zrecv[0] = tbuf[j, q]

            @pl.when(jnp.logical_not(mine))
            def _():
                remote(tbuf.at[j, q], zrecv.at[slot], S_PZ, R_PZ, (y * zs + other, 2 * x + q)).start()

    wait_bytes(e_z.at[pl.ds(0, zs - 1)], rcv.at[R_EZ])
    e_row = e_z[0]
    for d in range(1, zs):
        e_row = e_row + e_z[d]
    e_fin[s, y] = e_row
    for d in range(1, ys):
        remote(e_fin.at[s, y], e_fin.at[s, y], S_EA, R_EA, (((y + d) % ys) * zs + z, s)).start()

    wait_bytes(e_fin.at[0, pl.ds(0, ys - 1)], rcv.at[R_EA])
    for d in range(1, 2 * XS):
        remote(e_fin.at[s], e_fin.at[s], S_EF, R_EF, (dp, (s + d) % (2 * XS))).start()

    own_z = z // zh == c

    @pl.when(own_z)
    def _():
        wait_bytes(zrecv.at[pl.ds(0, zs - 1)], rcv.at[R_PZ])

    @pl.when(jnp.logical_not(own_z))
    def _():
        wait_bytes(zrecv, rcv.at[R_PZ])

    final = zrecv[0].astype(jnp.float32)
    for d in range(1, zs):
        final = final + zrecv[d].astype(jnp.float32)
    final = final / samples
    side = final[:own_rows]
    inner = final[tile // 2 : tile // 2 + own_rows]
    cut = quarter // 2 - LANES
    first_half = jnp.concatenate([side, inner[:, :cut]], axis=1)
    second_half = jnp.concatenate([inner[:, cut:], side], axis=1)
    pg_ref[...] = jnp.where(c == 0, first_half, second_half)

    wait_bytes(e_fin.at[pl.ds(0, 2 * XS - 1)], rcv.at[R_EF])
    for q in range(XS):
        at = slice(q * quarter, (q + 1) * quarter)
        for r in range(taps + 2):
            line = (e_fin[2 * q, r // e_rows, r % e_rows : r % e_rows + 1] + e_fin[2 * q + 1, r // e_rows, r % e_rows : r % e_rows + 1]) / samples
            if r < taps:
                kg_ref[r : r + 1, at] = line
            elif r == taps:
                bg_ref[at] = line.reshape(quarter)
            else:
                gg_ref[at] = line.reshape(quarter)

    wait_bytes(x_v.at[pl.ds(0, 2 * BLOCK)], snd.at[S_HALO])
    wait_bytes(cotg.at[pl.ds(0, 5)], snd.at[S_COT])
    wait_bytes(cotg.at[pl.ds(0, 2)], snd.at[S_FWD])
    wait_bytes(actc.at[pl.ds(0, 9)], snd.at[S_ACT])
    wait_bytes(actc, snd.at[S_SIB])
    wait_bytes(gb.at[pl.ds(0, 2 * BLOCK)], snd.at[S_GRAD])
    wait_bytes(e_x, snd.at[S_EX])
    wait_bytes(e_y, snd.at[S_EY])
    wait_bytes(e_z.at[pl.ds(0, zs - 1)], snd.at[S_EZ])
    wait_bytes(e_fin.at[0, pl.ds(0, ys - 1)], snd.at[S_EA])
    wait_bytes(e_fin.at[pl.ds(0, 2 * XS - 1)], snd.at[S_EF])

    @pl.when(own_y)
    def _():
        for k in range(CHUNKS):
            wait_bytes(pbuf.at[k, pl.ds(0, ys - 1)], snd.at[S_PY + k])

    @pl.when(jnp.logical_not(own_y))
    def _():
        for k in range(CHUNKS):
            wait_bytes(pbuf.at[k], snd.at[S_PY + k])
    put_ig.wait()

    @pl.when(own_z)
    def _():
        wait_bytes(zrecv.at[pl.ds(0, zs - 1)], snd.at[S_PZ])

    @pl.when(jnp.logical_not(own_z))
    def _():
        wait_bytes(zrecv, snd.at[S_PZ])


def put_kernel(ig_in, pg_in, kg_in, bg_in, gg_in, ig_out, pg_out, kg_out, bg_out, gg_out):
    ig_out[...] = ig_in[...]
    pg_out[...] = pg_in[...]
    kg_out[...] = kg_in[...]
    bg_out[...] = bg_in[...]
    gg_out[...] = gg_in[...]


def shards(ys, zs, section, lengths, taps, bias, gain, weight, cot, skip):
    samp, rows, chans = section.shape
    outs = cot.shape[2]
    half, quarter = outs // 2, chans // XS
    samples = ys * zs
    own_rows = outs // samples
    k_rows = own_rows * (zs // 2)
    tile = 2 * (-(-own_rows // 8) * 8)
    e_rows = HALO // ys
    kinds = taps.shape[0]
    bf16, f32 = jnp.bfloat16, jnp.float32
    vmem = pl.BlockSpec(memory_space=pltpu.VMEM)
    hbm = pl.BlockSpec(memory_space=pl.ANY)
    shapes = (
        jax.ShapeDtypeStruct((rows, chans), bf16),
        jax.ShapeDtypeStruct((own_rows, quarter // 2), f32),
        jax.ShapeDtypeStruct((kinds, chans), f32),
        jax.ShapeDtypeStruct((chans,), f32),
        jax.ShapeDtypeStruct((chans,), f32),
    )
    result = pl.pallas_call(
        functools.partial(kernel, ys, zs),
        out_shape=shapes,
        in_specs=[hbm] * 8,
        out_specs=(hbm,) + (vmem,) * 4,
        scratch_shapes=[
            pltpu.SMEM((samp,), jnp.int32),
            pltpu.VMEM((kinds, chans), f32),
            pltpu.VMEM((chans,), f32),
            pltpu.VMEM((chans,), f32),
            pltpu.VMEM((rows, chans), bf16),
            pltpu.VMEM((rows, outs), bf16),
            pltpu.VMEM((rows, chans), bf16),
            pltpu.VMEM((outs, chans), bf16),
            pltpu.VMEM((rows, chans), f32),
            pltpu.VMEM((BLOCK, chans), bf16),
            pltpu.VMEM((BLOCK, chans), bf16),
            pltpu.VMEM((rows + 2 * HALO, chans), f32),
            pltpu.VMEM((rows, chans), bf16),
            pltpu.VMEM((rows, chans), bf16),
            pltpu.VMEM((BLOCK, chans), bf16),
            pltpu.VMEM((BLOCK, chans), bf16),
            pltpu.VMEM((rows + 2 * HALO, chans), f32),
            pltpu.VMEM(((kinds + 2) * HALO, chans), f32),
            pltpu.VMEM((8, rows, half), bf16),
            pltpu.VMEM((half, 8 * rows), bf16),
            pltpu.VMEM((XS * CHUNKS, rows, LANES), bf16),
            pltpu.VMEM((CHUNKS, 8, rows, LANES), bf16),
            pltpu.VMEM((CHUNKS, half, LANES), f32),
            pltpu.VMEM((CHUNKS, ys, k_rows, LANES), bf16),
            pltpu.VMEM((CHUNKS, ys, k_rows, LANES), bf16),
            pltpu.VMEM((zs // 2, 2, tile, LANES), bf16),
            pltpu.VMEM((zs, tile, LANES), bf16),
            pltpu.VMEM((XS, HALO, quarter), f32),
            pltpu.VMEM((XS - 1, HALO, quarter), f32),
            pltpu.VMEM((ys, e_rows, quarter), f32),
            pltpu.VMEM((ys - 1, e_rows, quarter), f32),
            pltpu.VMEM((zs, e_rows, quarter), f32),
            pltpu.VMEM((2 * XS, ys, e_rows, quarter), f32),
            pltpu.SemaphoreType.DMA((11,)),
            pltpu.SemaphoreType.DMA((15,)),
            pltpu.SemaphoreType.DMA((29,)),
            pltpu.SemaphoreType.REGULAR((2,)),
            pltpu.SemaphoreType.REGULAR((3,)),
        ],
        compiler_params=pltpu.CompilerParams(collective_id=0, has_side_effects=True, vmem_limit_bytes=56 * 1024 * 1024),
        cost_estimate=pl.CostEstimate(flops=4 * rows * outs * chans, bytes_accessed=4_000_000, transcendentals=rows * chans),
    )(
        lengths,
        section.reshape(rows, chans),
        cot.reshape(rows, outs),
        skip.reshape(rows, chans),
        weight,
        taps,
        bias,
        gain,
    )
    result = pl.pallas_call(
        put_kernel,
        out_shape=shapes,
        in_specs=[vmem] * 5,
        out_specs=(vmem,) * 5,
        compiler_params=pltpu.CompilerParams(vmem_limit_bytes=56 * 1024 * 1024),
    )(result[0], result[1], result[2], result[3], result[4])
    return result[0].reshape(section.shape), result[1], result[2], result[3], result[4]


def solution(mesh):
    dp = mesh.shape["dp"]
    ys = 8 if dp == 128 else 2
    in_specs = (
        P("dp", "seq", None),
        P("dp"),
        P(),
        P(),
        P(),
        P(),
        P("dp", "seq", None),
        P("dp", "seq", None),
    )
    out_specs = (P("dp", "seq", None), P("dp", "seq"), P(), P(), P())
    return jax.shard_map(
        functools.partial(shards, ys, dp // ys), mesh=mesh, in_specs=in_specs, out_specs=out_specs, check_vma=False
    )
```

```python
import functools

import jax
import jax.numpy as jnp
from jax import lax
from jax.experimental import pallas as pl
from jax.experimental.pallas import tpu as pltpu
from jax.sharding import PartitionSpec as P

STEP = 4
MESH = pl.DeviceIdType.MESH
BLOCK = 16
HALO = 8
XS = 4
LANES = 128
ROOT = 0.7978845608028654
CUBIC = 0.044715

LOC_X, LOC_COT, LOC_SKIP, LOC_W, LOC_OWN, LOC_ACT, LOC_LEN, LOC_TAPS, LOC_BIAS, LOC_GAIN, LOC_IG = range(11)
(S_HALO, S_COT, S_FWD, S_ACT, S_SIB, S_GRAD, S_EX, S_EY, S_EZ, S_EA, S_EF, S_PZ) = range(12)
(R_TOP, R_BOT, R_COTS, R_COT1, R_COT2, R_COT3, R_GTOP, R_GBOT, R_EX, R_EY, R_EZ, R_EA, R_EF, R_PZ) = range(14)
S_PY = 12
R_ACT, R_SIB, R_PY = 14, 23, 26
CHUNKS = 3
ORDER = (1, 0, 2)


def wait_bytes(ref, sem):
    pltpu.make_async_copy(ref, ref, sem).wait()


def kernel(
    ys,
    zs,
    len_hbm,
    x_hbm,
    cot_hbm,
    skip_hbm,
    w_hbm,
    taps_hbm,
    bias_hbm,
    gain_hbm,
    ig_ref,
    pg_ref,
    kg_ref,
    bg_ref,
    gg_ref,
    len_ref,
    taps_ref,
    bias_ref,
    gain_ref,
    x_v,
    cot_v,
    skip_v,
    w_v,
    back,
    halo_t,
    halo_b,
    xpad,
    gb,
    ig_v,
    ghalo_t,
    ghalo_b,
    gpad,
    eacc,
    cotg,
    cott,
    actc,
    actg,
    pacc,
    pbuf,
    yrecv,
    tbuf,
    zrecv,
    e_loc,
    e_x,
    e_1,
    e_y,
    e_z,
    e_fin,
    loc,
    snd,
    rcv,
    ysem,
    zsem,
):
    rows, chans = x_v.shape
    outs = cot_v.shape[1]
    half = outs // 2
    quarter = chans // XS
    taps = taps_ref.shape[0]
    samples = ys * zs
    own_rows = outs // samples
    yh, zh = ys // 2, zs // 2
    k_rows = own_rows * zh
    tile = tbuf.shape[2]
    e_rows = e_1.shape[1]

    dp = lax.axis_index("dp")
    s = lax.axis_index("seq")
    y, z = dp // zs, dp % zs
    x, c = s // 2, s % 2
    oc = 1 - c
    sib = 2 * x + oc

    def xat(delta, core):
        return (dp, 2 * ((x + delta) % XS) + core)

    def remote(src, dst, send, recv, device):
        return pltpu.make_async_remote_copy(
            src_ref=src, dst_ref=dst, send_sem=snd.at[send], recv_sem=rcv.at[recv], device_id=device, device_id_type=MESH
        )

    ld_x = pltpu.make_async_copy(x_hbm, x_v, loc.at[LOC_X])
    ld_cot = pltpu.make_async_copy(cot_hbm, cot_v, loc.at[LOC_COT])
    ld_w = pltpu.make_async_copy(w_hbm, w_v, loc.at[LOC_W])
    ld_skip = pltpu.make_async_copy(skip_hbm, skip_v, loc.at[LOC_SKIP])
    my_half = pl.multiple_of(c * half, LANES)
    ld_own = pltpu.make_async_copy(cot_hbm.at[:, pl.ds(my_half, half)], cotg.at[0], loc.at[LOC_OWN])
    ld_x.start()
    ld_cot.start()
    ld_w.start()
    ld_skip.start()
    ld_own.start()
    ld_len = pltpu.make_async_copy(len_hbm, len_ref, loc.at[LOC_LEN])
    ld_taps = pltpu.make_async_copy(taps_hbm, taps_ref, loc.at[LOC_TAPS])
    ld_bias = pltpu.make_async_copy(bias_hbm, bias_ref, loc.at[LOC_BIAS])
    ld_gain = pltpu.make_async_copy(gain_hbm, gain_ref, loc.at[LOC_GAIN])
    ld_len.start()
    ld_taps.start()
    ld_bias.start()
    ld_gain.start()

    barrier = pltpu.get_barrier_semaphore()
    for d in range(1, 2 * XS):
        pl.semaphore_signal(barrier, inc=1, device_id=(dp, (s + d) % (2 * XS)), device_id_type=MESH)
    y_steps = (1, ys - 1) if ys > 2 else (1,)
    z_steps = (1, zs - 1) if zs > 2 else (1,)
    for d in y_steps:
        for device in (s, sib):
            pl.semaphore_signal(barrier, inc=1, device_id=(((y + d) % ys) * zs + z, device), device_id_type=MESH)
    for d in z_steps:
        for device in (s, sib):
            pl.semaphore_signal(barrier, inc=1, device_id=(y * zs + (z + d) % zs, device), device_id_type=MESH)
    pl.semaphore_wait(barrier, 2 * XS - 1 + 2 * (1 if ys == 2 else 2) + 2 * (1 if zs == 2 else 2))

    reach_y = (1, 2) if ys == 8 else ()
    reach_z = (1, 2, 4) if zs == 16 else (1,) if zs == 4 else ()

    def tell(i):
        if i < len(reach_y):
            for d in (reach_y[i], ys - reach_y[i]):
                pl.semaphore_signal(ysem.at[i], inc=1, device_id=(((y + d) % ys) * zs + z, s), device_id_type=MESH)
        if i < len(reach_z):
            for d in (reach_z[i], zs - reach_z[i]):
                pl.semaphore_signal(zsem.at[i], inc=1, device_id=(y * zs + (z + d) % zs, s), device_id_type=MESH)

    def hear(i):
        if i < len(reach_y):
            pl.semaphore_wait(ysem.at[i], 2)
        if i < len(reach_z):
            pl.semaphore_wait(zsem.at[i], 2)

    up, down = (dp, (s + 1) % (2 * XS)), (dp, (s + 2 * XS - 1) % (2 * XS))
    remote(x_hbm.at[pl.ds(rows - BLOCK, BLOCK)], halo_t, S_HALO, R_TOP, up).start()
    remote(x_hbm.at[pl.ds(0, BLOCK)], halo_b, S_HALO, R_BOT, down).start()

    for delta, recv in ((1, R_COT3), (3, R_COT1), (0, R_COTS)):
        for p in (0, 1):
            if delta == 0 and p == 0:
                continue
            core = c if p == 0 else oc
            start = pl.multiple_of(core * half, LANES)
            remote(
                cot_hbm.at[:, pl.ds(start, half)], cotg.at[4 * p + (XS - delta) % XS], S_COT, recv, xat(delta, core)
            ).start()
    tell(0)

    ld_len.wait()
    length = len_ref[0]
    first = s * rows
    row_id = lax.broadcasted_iota(jnp.int32, (BLOCK, 1), 0)

    ld_cot.wait()
    ld_w.wait()
    ld_skip.wait()

    def back_step(i, carry):
        at = pl.ds(pl.multiple_of(i * quarter, LANES), quarter)
        back[:, at] = jnp.dot(cot_v[...], w_v[:, at], preferred_element_type=jnp.float32) + skip_v[:, at].astype(jnp.float32)
        return carry

    hear(0)
    tell(1)
    lax.fori_loop(0, XS, back_step, 0)

    ld_x.wait()
    ld_taps.wait()
    ld_bias.wait()
    ld_gain.wait()

    def mask_step(i, carry):
        r0 = pl.multiple_of(i * BLOCK, BLOCK)
        value = x_v[pl.ds(r0, BLOCK), :].astype(jnp.float32)
        xpad[pl.ds(r0 + HALO, BLOCK), :] = jnp.where(first + r0 + row_id < length, value, 0.0)
        return carry

    lax.fori_loop(0, rows // BLOCK, mask_step, 0)
    eacc[...] = jnp.zeros_like(eacc)

    wait_bytes(halo_t, rcv.at[R_TOP])
    wait_bytes(halo_b, rcv.at[R_BOT])
    head_id = first - HALO + lax.broadcasted_iota(jnp.int32, (HALO, 1), 0)
    head = halo_t[...].astype(jnp.float32)[BLOCK - HALO :]
    xpad[0:HALO, :] = jnp.where(jnp.logical_and(head_id >= 0, head_id < length), head, 0.0)
    tail_id = first + rows + lax.broadcasted_iota(jnp.int32, (HALO, 1), 0)
    tail = halo_b[...].astype(jnp.float32)[:HALO]
    xpad[pl.ds(rows + HALO, HALO), :] = jnp.where(
        jnp.logical_and(tail_id < length, s < 2 * XS - 1), tail, 0.0
    )

    def fold(value):
        return value[:HALO] + value[HALO:]

    def shifted(ref, r0):
        even = ref[pl.ds(r0, 2 * BLOCK), :]
        odd = even[STEP : STEP + BLOCK + HALO]
        return [even[:BLOCK], odd[:BLOCK], even[HALO : HALO + BLOCK], odd[HALO:], even[BLOCK:]]

    def main_step(i, carry):
        r0 = pl.multiple_of(i * BLOCK, BLOCK)
        seen = shifted(xpad, r0)
        hidden = bias_ref[...].reshape(1, chans) + taps_ref[0:1, :] * seen[0]
        for j in range(1, taps):
            hidden = hidden + taps_ref[j : j + 1, :] * seen[j]
        inverse = lax.rsqrt(jnp.mean(hidden * hidden, axis=-1, keepdims=True) + 1e-06)
        normed = hidden * inverse
        gain = gain_ref[...].reshape(1, chans)
        u = normed * gain
        square = u * u
        tanh = jnp.tanh(u * (ROOT + ROOT * CUBIC * square))
        cdf = 0.5 + 0.5 * tanh
        act = (u * cdf).astype(jnp.bfloat16)
        for m in range(XS * CHUNKS):
            actc[m, pl.ds(r0, BLOCK), :] = act[:, m * LANES : (m + 1) * LANES]
        slope = cdf + u * (1.0 - tanh * tanh) * (0.5 * ROOT + 1.5 * ROOT * CUBIC * square)
        toward = back[pl.ds(r0, BLOCK), :] * slope
        eacc[pl.ds((taps + 1) * HALO, HALO), :] += fold(toward * normed)
        toward = toward * gain
        pull = jnp.mean(toward * normed, axis=-1, keepdims=True)
        grad = ((toward - normed * pull) * inverse).astype(jnp.bfloat16)
        gb[pl.ds(r0, BLOCK), :] = grad
        grad = grad.astype(jnp.float32)
        gpad[pl.ds(r0 + HALO, BLOCK), :] = grad
        eacc[pl.ds(taps * HALO, HALO), :] += fold(grad)
        for j in range(taps):
            eacc[pl.ds(j * HALO, HALO), :] += fold(grad * seen[j])
        return carry

    lax.fori_loop(0, rows // BLOCK, main_step, 0)

    for r in range(taps + 2):
        line = jnp.sum(eacc[r * HALO : (r + 1) * HALO, :], axis=0, keepdims=True)
        for q in range(XS):
            e_loc[q, r : r + 1, :] = line[:, q * quarter : (q + 1) * quarter]
    for q in range(XS):
        e_loc[q, taps + 2 :, :] = jnp.zeros((HALO - taps - 2, quarter), jnp.float32)
    for delta in (2, 1, 3):
        remote(e_loc.at[(x + delta) % XS], e_x.at[XS - delta - 1], S_EX, R_EX, xat(delta, c)).start()

    remote(gb.at[pl.ds(rows - BLOCK, BLOCK)], ghalo_t, S_GRAD, R_GTOP, up).start()
    remote(gb.at[pl.ds(0, BLOCK)], ghalo_b, S_GRAD, R_GBOT, down).start()

    part = rows // 2
    wait_bytes(cotg.at[pl.ds(0, 2)], rcv.at[R_COT3])
    for p in (0, 1):
        at = pl.ds(0, part)
        remote(cotg.at[4 * p + 3, at], cotg.at[4 * p + 2, at], S_FWD, R_COT2, xat(1, c)).start()
    wait_bytes(cotg.at[pl.ds(0, 2)], rcv.at[R_COT1])
    for p in (0, 1):
        at = pl.ds(part, part)
        remote(cotg.at[4 * p + 1, at], cotg.at[4 * p + 2, at], S_FWD, R_COT2, xat(3, c)).start()

    for k in ORDER:
        for delta in (2, 1, 3):
            slot = XS - delta
            remote(
                actc.at[CHUNKS * ((x + delta) % XS) + k], actg.at[k, slot], S_ACT, R_ACT + 3 * k + slot - 1, xat(delta, c)
            ).start()
        remote(actc.at[CHUNKS * x + k], actg.at[k, 4], S_SIB, R_SIB + k, (dp, sib)).start()
        pltpu.make_async_copy(actc.at[CHUNKS * x + k], actg.at[k, 0], loc.at[LOC_ACT]).start()
    hear(1)
    tell(2)

    def turn(slot):
        cott[:, slot * rows : (slot + 1) * rows] = jnp.transpose(cotg[slot])

    ld_own.wait()
    wait_bytes(cotg.at[0], rcv.at[R_COTS])
    for slot in (0, 4, 1, 5, 3, 7):
        turn(slot)

    wait_bytes(ghalo_t, rcv.at[R_GTOP])
    wait_bytes(ghalo_b, rcv.at[R_GBOT])
    gpad[0:HALO, :] = jnp.where(s > 0, ghalo_t[...].astype(jnp.float32)[BLOCK - HALO :], 0.0)
    gpad[pl.ds(rows + HALO, HALO), :] = jnp.where(s < 2 * XS - 1, ghalo_b[...].astype(jnp.float32)[:HALO], 0.0)

    def input_step(i, carry):
        r0 = pl.multiple_of(i * BLOCK, BLOCK)
        seen = shifted(gpad, r0)
        total = taps_ref[0:1, :] * seen[taps - 1]
        for j in range(1, taps):
            total = total + taps_ref[j : j + 1, :] * seen[taps - 1 - j]
        ig_v[pl.ds(r0, BLOCK), :] = jnp.where(first + r0 + row_id < length, total, 0.0).astype(jnp.bfloat16)
        return carry

    lax.fori_loop(0, rows // BLOCK, input_step, 0)
    put_ig = pltpu.make_async_copy(ig_v, ig_ref, loc.at[LOC_IG])
    put_ig.start()
    hear(2)

    wait_bytes(e_x, rcv.at[R_EX])
    e_sum = e_loc[x] + e_x[0] + e_x[1] + e_x[2]
    for r in range(HALO):
        e_1[r // e_rows, r % e_rows : r % e_rows + 1, :] = e_sum[r : r + 1]
    for d in range(1, ys):
        other = (y + d) % ys
        remote(e_1.at[other], e_y.at[ys - d - 1], S_EY, R_EY, (other * zs + z, s)).start()

    wait_bytes(cotg.at[pl.ds(0, 2)], rcv.at[R_COT2])
    turn(2)
    turn(6)
    wait_bytes(actc.at[pl.ds(0, CHUNKS)], loc.at[LOC_ACT])

    def same_parity(k):
        for d in (1, 3, 2):
            wait_bytes(actg.at[k, d], rcv.at[R_ACT + 3 * k + d - 1])
            remote(actg.at[k, d], actg.at[k, 4 + d], S_SIB, R_SIB + k, (dp, sib)).start()
        pacc[k] = jnp.dot(
            cott[:, : 4 * rows], actg[k, 0:4].reshape(4 * rows, LANES), preferred_element_type=jnp.float32
        )

    def other_parity(k):
        wait_bytes(actg.at[k, pl.ds(4, 4)], rcv.at[R_SIB + k])
        whole = pacc[k] + jnp.dot(
            cott[:, 4 * rows :], actg[k, 4:8].reshape(4 * rows, LANES), preferred_element_type=jnp.float32
        )
        whole = whole.astype(jnp.bfloat16)
        for i in range(ys):
            pbuf[k, i] = whole[i * k_rows : (i + 1) * k_rows]
        for i in range(yh):
            for core in range(2):
                turn_i = (y + i) % yh
                other = yh * c + turn_i
                slot = (y + ys - other) % ys
                mine = jnp.logical_and(other == y, c == core)

                @pl.when(mine)
                def _():
                    yrecv[k, 0] = pbuf[k, 2 * turn_i + core]

                @pl.when(jnp.logical_not(mine))
                def _():
                    remote(
                        pbuf.at[k, 2 * turn_i + core], yrecv.at[k, slot], S_PY + k, R_PY + k, (other * zs + z, 2 * x + core)
                    ).start()

    def small_over_y():
        wait_bytes(e_y, rcv.at[R_EY])
        e_row = e_1[y]
        for d in range(ys - 1):
            e_row = e_row + e_y[d]
        e_z[z] = e_row
        for d in range(1, zs):
            remote(e_z.at[z], e_z.at[z], S_EZ, R_EZ, (y * zs + (z + d) % zs, s)).start()

    def small_over_z():
        wait_bytes(e_z.at[pl.ds(0, zs - 1)], rcv.at[R_EZ])
        e_row = e_z[0]
        for d in range(1, zs):
            e_row = e_row + e_z[d]
        e_fin[s, y] = e_row
        for d in range(1, ys):
            remote(e_fin.at[s, y], e_fin.at[s, y], S_EA, R_EA, (((y + d) % ys) * zs + z, s)).start()

    def small_to_all():
        wait_bytes(e_fin.at[0, pl.ds(0, ys - 1)], rcv.at[R_EA])
        for d in range(1, 2 * XS):
            remote(e_fin.at[s], e_fin.at[s], S_EF, R_EF, (dp, (s + d) % (2 * XS))).start()

    same_parity(ORDER[0])
    small_over_y()
    same_parity(ORDER[1])
    other_parity(ORDER[0])
    same_parity(ORDER[2])
    other_parity(ORDER[1])
    other_parity(ORDER[2])

    own_y = y // yh == c
    sel_row = lax.broadcasted_iota(jnp.int32, (zh * tile, k_rows), 0)
    sel_col = lax.broadcasted_iota(jnp.int32, (zh * tile, k_rows), 1)
    within = sel_row % tile
    base = (sel_row // tile) * own_rows
    pick_a = jnp.logical_and(within < own_rows, sel_col == base + within).astype(jnp.bfloat16)
    low = within - tile // 2
    pick_b = jnp.logical_and(jnp.logical_and(low >= 0, low < own_rows), sel_col == base + low).astype(jnp.bfloat16)

    def over_y(k, pick):
        @pl.when(own_y)
        def _():
            wait_bytes(yrecv.at[k, pl.ds(0, ys - 1)], rcv.at[R_PY + k])

        @pl.when(jnp.logical_not(own_y))
        def _():
            wait_bytes(yrecv.at[k], rcv.at[R_PY + k])

        total = yrecv[k, 0].astype(jnp.float32)
        for d in range(1, ys):
            total = total + yrecv[k, d].astype(jnp.float32)
        return jnp.dot(pick, total.astype(jnp.bfloat16), preferred_element_type=jnp.float32)

    small_over_z()
    middle = over_y(1, pick_b)
    for q in range(2):
        if q == 1:
            small_to_all()
        both = (over_y(2 * q, pick_a) + middle).astype(jnp.bfloat16)
        for j in range(zh):
            tbuf[j, q] = both[j * tile : (j + 1) * tile]
        for j in range(zh):
            turn_j = (z + j) % zh
            other = zh * c + turn_j
            slot = (z + zs - other) % zs
            mine = jnp.logical_and(other == z, c == q)

            @pl.when(mine)
            def _():
                zrecv[0] = tbuf[turn_j, q]

            @pl.when(jnp.logical_not(mine))
            def _():
                remote(tbuf.at[turn_j, q], zrecv.at[slot], S_PZ, R_PZ, (y * zs + other, 2 * x + q)).start()

    wait_bytes(e_fin.at[pl.ds(0, 2 * XS - 1)], rcv.at[R_EF])
    for q in range(XS):
        at = slice(q * quarter, (q + 1) * quarter)
        for r in range(taps + 2):
            line = (e_fin[2 * q, r // e_rows, r % e_rows : r % e_rows + 1] + e_fin[2 * q + 1, r // e_rows, r % e_rows : r % e_rows + 1]) / samples
            if r < taps:
                kg_ref[r : r + 1, at] = line
            elif r == taps:
                bg_ref[at] = line.reshape(quarter)
            else:
                gg_ref[at] = line.reshape(quarter)

    own_z = z // zh == c

    @pl.when(own_z)
    def _():
        wait_bytes(zrecv.at[pl.ds(0, zs - 1)], rcv.at[R_PZ])

    @pl.when(jnp.logical_not(own_z))
    def _():
        wait_bytes(zrecv, rcv.at[R_PZ])

    final = zrecv[0].astype(jnp.float32)
    for d in range(1, zs):
        final = final + zrecv[d].astype(jnp.float32)
    final = final / samples
    side = final[:own_rows]
    inner = final[tile // 2 : tile // 2 + own_rows]
    cut = quarter // 2 - LANES
    first_half = jnp.concatenate([side, inner[:, :cut]], axis=1)
    second_half = jnp.concatenate([inner[:, cut:], side], axis=1)
    pg_ref[...] = jnp.where(c == 0, first_half, second_half)

    wait_bytes(x_v.at[pl.ds(0, 2 * BLOCK)], snd.at[S_HALO])
    wait_bytes(cotg.at[pl.ds(0, 5)], snd.at[S_COT])
    wait_bytes(cotg.at[pl.ds(0, 2)], snd.at[S_FWD])
    wait_bytes(actc.at[pl.ds(0, 9)], snd.at[S_ACT])
    wait_bytes(actc, snd.at[S_SIB])
    wait_bytes(gb.at[pl.ds(0, 2 * BLOCK)], snd.at[S_GRAD])
    wait_bytes(e_x, snd.at[S_EX])
    wait_bytes(e_y, snd.at[S_EY])
    wait_bytes(e_z.at[pl.ds(0, zs - 1)], snd.at[S_EZ])
    wait_bytes(e_fin.at[0, pl.ds(0, ys - 1)], snd.at[S_EA])
    wait_bytes(e_fin.at[pl.ds(0, 2 * XS - 1)], snd.at[S_EF])

    @pl.when(own_y)
    def _():
        for k in range(CHUNKS):
            wait_bytes(pbuf.at[k, pl.ds(0, ys - 1)], snd.at[S_PY + k])

    @pl.when(jnp.logical_not(own_y))
    def _():
        for k in range(CHUNKS):
            wait_bytes(pbuf.at[k], snd.at[S_PY + k])
    put_ig.wait()

    @pl.when(own_z)
    def _():
        wait_bytes(zrecv.at[pl.ds(0, zs - 1)], snd.at[S_PZ])

    @pl.when(jnp.logical_not(own_z))
    def _():
        wait_bytes(zrecv, snd.at[S_PZ])


def put_kernel(ig_in, pg_in, kg_in, bg_in, gg_in, ig_out, pg_out, kg_out, bg_out, gg_out):
    ig_out[...] = ig_in[...]
    pg_out[...] = pg_in[...]
    kg_out[...] = kg_in[...]
    bg_out[...] = bg_in[...]
    gg_out[...] = gg_in[...]


def shards(ys, zs, section, lengths, taps, bias, gain, weight, cot, skip):
    samp, rows, chans = section.shape
    outs = cot.shape[2]
    half, quarter = outs // 2, chans // XS
    samples = ys * zs
    own_rows = outs // samples
    k_rows = own_rows * (zs // 2)
    tile = 2 * (-(-own_rows // 8) * 8)
    e_rows = HALO // ys
    kinds = taps.shape[0]
    bf16, f32 = jnp.bfloat16, jnp.float32
    vmem = pl.BlockSpec(memory_space=pltpu.VMEM)
    hbm = pl.BlockSpec(memory_space=pl.ANY)
    shapes = (
        jax.ShapeDtypeStruct((rows, chans), bf16),
        jax.ShapeDtypeStruct((own_rows, quarter // 2), f32),
        jax.ShapeDtypeStruct((kinds, chans), f32),
        jax.ShapeDtypeStruct((chans,), f32),
        jax.ShapeDtypeStruct((chans,), f32),
    )
    result = pl.pallas_call(
        functools.partial(kernel, ys, zs),
        out_shape=shapes,
        in_specs=[hbm] * 8,
        out_specs=(hbm,) + (vmem,) * 4,
        scratch_shapes=[
            pltpu.SMEM((samp,), jnp.int32),
            pltpu.VMEM((kinds, chans), f32),
            pltpu.VMEM((chans,), f32),
            pltpu.VMEM((chans,), f32),
            pltpu.VMEM((rows, chans), bf16),
            pltpu.VMEM((rows, outs), bf16),
            pltpu.VMEM((rows, chans), bf16),
            pltpu.VMEM((outs, chans), bf16),
            pltpu.VMEM((rows, chans), f32),
            pltpu.VMEM((BLOCK, chans), bf16),
            pltpu.VMEM((BLOCK, chans), bf16),
            pltpu.VMEM((rows + 2 * HALO, chans), f32),
            pltpu.VMEM((rows, chans), bf16),
            pltpu.VMEM((rows, chans), bf16),
            pltpu.VMEM((BLOCK, chans), bf16),
            pltpu.VMEM((BLOCK, chans), bf16),
            pltpu.VMEM((rows + 2 * HALO, chans), f32),
            pltpu.VMEM(((kinds + 2) * HALO, chans), f32),
            pltpu.VMEM((8, rows, half), bf16),
            pltpu.VMEM((half, 8 * rows), bf16),
            pltpu.VMEM((XS * CHUNKS, rows, LANES), bf16),
            pltpu.VMEM((CHUNKS, 8, rows, LANES), bf16),
            pltpu.VMEM((CHUNKS, half, LANES), f32),
            pltpu.VMEM((CHUNKS, ys, k_rows, LANES), bf16),
            pltpu.VMEM((CHUNKS, ys, k_rows, LANES), bf16),
            pltpu.VMEM((zs // 2, 2, tile, LANES), bf16),
            pltpu.VMEM((zs, tile, LANES), bf16),
            pltpu.VMEM((XS, HALO, quarter), f32),
            pltpu.VMEM((XS - 1, HALO, quarter), f32),
            pltpu.VMEM((ys, e_rows, quarter), f32),
            pltpu.VMEM((ys - 1, e_rows, quarter), f32),
            pltpu.VMEM((zs, e_rows, quarter), f32),
            pltpu.VMEM((2 * XS, ys, e_rows, quarter), f32),
            pltpu.SemaphoreType.DMA((11,)),
            pltpu.SemaphoreType.DMA((15,)),
            pltpu.SemaphoreType.DMA((29,)),
            pltpu.SemaphoreType.REGULAR((2,)),
            pltpu.SemaphoreType.REGULAR((3,)),
        ],
        compiler_params=pltpu.CompilerParams(collective_id=0, has_side_effects=True, vmem_limit_bytes=56 * 1024 * 1024),
        cost_estimate=pl.CostEstimate(flops=4 * rows * outs * chans, bytes_accessed=4_000_000, transcendentals=rows * chans),
    )(
        lengths,
        section.reshape(rows, chans),
        cot.reshape(rows, outs),
        skip.reshape(rows, chans),
        weight,
        taps,
        bias,
        gain,
    )
    result = pl.pallas_call(
        put_kernel,
        out_shape=shapes,
        in_specs=[vmem] * 5,
        out_specs=(vmem,) * 5,
        compiler_params=pltpu.CompilerParams(vmem_limit_bytes=56 * 1024 * 1024),
    )(result[0], result[1], result[2], result[3], result[4])
    return result[0].reshape(section.shape), result[1], result[2], result[3], result[4]


def solution(mesh):
    dp = mesh.shape["dp"]
    ys = 8 if dp == 128 else 2
    in_specs = (
        P("dp", "seq", None),
        P("dp"),
        P(),
        P(),
        P(),
        P(),
        P("dp", "seq", None),
        P("dp", "seq", None),
    )
    out_specs = (P("dp", "seq", None), P("dp", "seq"), P(), P(), P())
    return jax.shard_map(
        functools.partial(shards, ys, dp // ys), mesh=mesh, in_specs=in_specs, out_specs=out_specs, check_vma=False
    )
```
